512 devices in a mesh: row: 16 (over y, core), col: 32 (over z, x).
Axes of the slice: x: 4, y: 8, z: 8, core: 2. Of those that a mesh axis runs over, the one named last changes fastest.
Arguments:
- inputs: bfloat16 [768, 8192], P('col', 'row'), may hold values from -6 to 6
- w_gate: bfloat16 [8192, 14336], P('row', 'col'), may hold values from -0.0625 to 0.0625
- w_up: bfloat16 [8192, 14336], P('row', 'col'), may hold values from -0.0625 to 0.0625
- w_down: bfloat16 [14336, 8192], P('col', 'row'), may hold values from -0.046875 to 0.046875
- cotangent: bfloat16 [768, 8192], P('col', 'row'), may hold values from -6 to 6
Outputs:
- grad_inputs: bfloat16 [768, 8192], P('col', 'row')
- grad_gate: bfloat16 [8192, 14336], P('row', 'col')
- grad_up: bfloat16 [8192, 14336], P('row', 'col')
- grad_down: bfloat16 [14336, 8192], P('col', 'row')
The draws below stay inside these ranges and needn't reach their ends.
All inputs are finite; a program needn't handle non-finite values.
Results may differ from the reference program's by a relative error of at most 0.0049.
Values may be sent and summed in bfloat16 or wider, within the bound.
No kernel may reach another device: no remote copies, remote signals or barrier semaphores. Data moves between devices by JAX's collectives and lax.ppermute only.
A program may use at most 64 MiB of HBM per device.

```python
import jax
import jax.numpy as jnp

D = 8192
FF_WIN = 14336
TOKENS = 768


def shard_levels(key, dims, cuts, smallest, high):
    gain, own = 1.0, jax.random.fold_in(key, 6)
    for axis_at, parts in cuts:
        draws = jnp.exp(jax.random.uniform(jax.random.fold_in(own, axis_at), (parts,), jnp.float32, smallest / len(cuts), high / len(cuts)))
        gain = gain * jnp.repeat(draws, dims[axis_at] // parts).reshape([-1 if axis == axis_at else 1 for axis in range(len(dims))])
    return gain


def bell_draw(key, extent, scale, most, cuts=(), held_as=jnp.bfloat16):
    factor_of = shard_levels(key, extent, cuts, -0.22, 0.18) if cuts else 1.0
    values = jax.random.normal(key, extent, jnp.float32) * scale * factor_of
    return jnp.minimum(jnp.maximum(values, -most), most).astype(held_as)


def setup_inputs(seed: int = 0) -> dict:
    arg_keys = jax.random.split(jax.random.key(seed), 6)
    return {
        "inputs": bell_draw(arg_keys[0], (TOKENS, D), 1.0, 6.0, ((0, 32), (1, 16))),
        "w_gate": bell_draw(arg_keys[1], (D, FF_WIN), D ** -0.5, 0.0625, ((0, 16), (1, 32))),
        "w_up": bell_draw(arg_keys[2], (D, FF_WIN), D ** -0.5, 0.0625, ((0, 16), (1, 32))),
        "w_down": bell_draw(arg_keys[3], (FF_WIN, D), FF_WIN ** -0.5, 0.046875, ((0, 32), (1, 16))),
        "cotangent": bell_draw(arg_keys[4], (TOKENS, D), 1.0, 6.0, ((0, 32), (1, 16))),
    }


def reference(inputs, w_gate, w_up, w_down, cotangent):
    gate_sum = jnp.dot(inputs, w_gate, preferred_element_type=jnp.float32)
    up_sum = jnp.dot(inputs, w_up, preferred_element_type=jnp.float32)
    grad_hidden = jnp.dot(cotangent, w_down.T, preferred_element_type=jnp.float32)
    sigmoid_gate = jax.nn.sigmoid(gate_sum)
    activated = gate_sum * sigmoid_gate
    hidden = (activated * up_sum).astype(jnp.bfloat16)
    grad_gate_act = (grad_hidden * up_sum * sigmoid_gate * (1.0 + gate_sum * (1.0 - sigmoid_gate))).astype(jnp.bfloat16)
    grad_up_act = (grad_hidden * activated).astype(jnp.bfloat16)
    grad_inputs = (jnp.dot(grad_gate_act, w_gate.T, preferred_element_type=jnp.float32)
                   + jnp.dot(grad_up_act, w_up.T, preferred_element_type=jnp.float32)).astype(jnp.bfloat16)
    grad_gate = jnp.dot(inputs.T, grad_gate_act, preferred_element_type=jnp.float32).astype(jnp.bfloat16)
    grad_up = jnp.dot(inputs.T, grad_up_act, preferred_element_type=jnp.float32).astype(jnp.bfloat16)
    grad_down = jnp.dot(hidden.T, cotangent, preferred_element_type=jnp.float32).astype(jnp.bfloat16)
    return grad_inputs, grad_gate, grad_up, grad_down
```

```python
import jax
import jax.numpy as jnp
from jax import lax
from jax.sharding import Mesh, PartitionSpec as P

F32 = jnp.float32
BF16 = jnp.bfloat16


def dot(left, right, left_dim, right_dim):
    return lax.dot_general(
        left, right, (((left_dim,), (right_dim,)), ((), ())), preferred_element_type=F32
    )


def spread(block, axis, size):
    copies = jnp.broadcast_to(block[None], (size, *block.shape))
    return lax.all_to_all(copies, axis, 0, 0)


def build(sizes):
    ny, nc, nz, nx = sizes

    def on_device(inputs, w_gate, w_up, w_down, cotangent):
        width, columns = w_gate.shape
        rows = inputs.shape[0]
        tokens = rows * nz * nx
        half = tokens // nc
        both = jnp.concatenate([inputs, cotangent], axis=1)
        along_z = spread(both, "z", nz).reshape(nz * rows, 2 * width)
        held = spread(along_z, "x", nx).reshape(tokens, 2 * width)

        core = lax.axis_index("c")

        def partial_sums(block):
            return jnp.concatenate(
                [
                    dot(block[:, :width], w_gate, 1, 0),
                    dot(block[:, :width], w_up, 1, 0),
                    dot(block[:, width:], w_down, 1, 1),
                ],
                axis=1,
            )

        other = lax.dynamic_slice_in_dim(held, (1 - core) * half, half, 0)
        mine = lax.dynamic_slice_in_dim(held, core * half, half, 0)
        received = lax.ppermute(partial_sums(other), "c", [(0, 1), (1, 0)])
        chip_sums = (partial_sums(mine) + received).astype(BF16)
        parts = lax.all_to_all(
            chip_sums.reshape(ny, half // ny, 3 * columns), "y", 0, 0
        )
        summed = jnp.sum(parts.astype(F32), axis=0)
        gate_sum = summed[:, :columns]
        up_sum = summed[:, columns : 2 * columns]
        grad_hidden = summed[:, 2 * columns :]
        sigmoid_gate = jax.nn.sigmoid(gate_sum)
        activated = gate_sum * sigmoid_gate
        pieces = jnp.concatenate(
            [
                grad_hidden * up_sum * sigmoid_gate * (1.0 + gate_sum * (1.0 - sigmoid_gate)),
                grad_hidden * activated,
                activated * up_sum,
            ],
            axis=1,
        ).astype(BF16)
        pieces = lax.all_gather(pieces, "y", axis=0, tiled=True)
        pieces = lax.all_gather(pieces, "c", axis=0, tiled=True)
        grad_gate_act = pieces[:, :columns]
        grad_up_act = pieces[:, columns : 2 * columns]
        hidden = pieces[:, 2 * columns :]

        share = dot(grad_gate_act, w_gate, 1, 1) + dot(grad_up_act, w_up, 1, 1)
        shares = lax.all_to_all(
            share.astype(BF16).reshape(nx * nz, rows, width), ("x", "z"), 0, 0
        )
        grad_inputs = jnp.sum(shares.astype(F32), axis=0).astype(BF16)
        all_inputs, all_cotangent = held[:, :width], held[:, width:]
        return (
            grad_inputs,
            dot(all_inputs, grad_gate_act, 0, 0).astype(BF16),
            dot(all_inputs, grad_up_act, 0, 0).astype(BF16),
            dot(hidden, all_cotangent, 0, 0).astype(BF16),
        )

    return on_device


def solution(mesh):
    row, col = mesh.devices.shape
    sizes = (row // 2, 2, col // 4, 4)
    fine = Mesh(mesh.devices.reshape(sizes), ("y", "c", "z", "x"))
    token_width, width_hidden, hidden_width = (
        P(("z", "x"), ("y", "c")),
        P(("y", "c"), ("z", "x")),
        P(("z", "x"), ("y", "c")),
    )
    return jax.shard_map(
        build(sizes),
        mesh=fine,
        in_specs=(token_width, width_hidden, width_hidden, hidden_width, token_width),
        out_specs=(token_width, width_hidden, width_hidden, hidden_width),
        check_vma=False,
    )
```

```python
import functools

import jax
import jax.numpy as jnp
from jax import lax
from jax.experimental import pallas as pl
from jax.experimental.pallas import tpu as pltpu
from jax.sharding import Mesh, PartitionSpec as P

F32 = jnp.float32
BF16 = jnp.bfloat16
SWAP = [(0, 1), (1, 0)]


def dot(left, right, left_dim, right_dim):
    return lax.dot_general(
        left, right, (((left_dim,), (right_dim,)), ((), ())), preferred_element_type=F32
    )


def sibling(value):
    return lax.ppermute(value, "c", SWAP)


def spread(block, axis, size):
    copies = jnp.broadcast_to(block[None], (size, *block.shape))
    return lax.all_to_all(copies, axis, 0, 0)


def after(value, *earlier):
    return lax.optimization_barrier((value, *earlier))[0]


def local(kernel, out_shape, flops, moved, core, *operands):
    return pl.pallas_call(
        kernel,
        out_shape=out_shape,
        in_specs=[pl.BlockSpec(memory_space=pltpu.SMEM)]
        + [pl.BlockSpec(memory_space=pltpu.VMEM)] * len(operands),
        out_specs=jax.tree.map(lambda _: pl.BlockSpec(memory_space=pltpu.VMEM), out_shape),
        compiler_params=pltpu.CompilerParams(vmem_limit_bytes=24 * 1024 * 1024),
        cost_estimate=pl.CostEstimate(flops=flops, bytes_accessed=moved, transcendentals=0),
    )(core.reshape(1).astype(jnp.int32), *operands)


def sums_kernel(count, flip, core_ref, block_ref, *refs):
    weights, rest = refs[:count], refs[count:]
    out_ref = rest[-1]
    half = block_ref.shape[0] // 2
    side = 1 - core_ref[0] if flip else core_ref[0]
    block = block_ref[pl.ds(pl.multiple_of(side * half, half), half), :]
    ny, rows = out_ref.shape[0], out_ref.shape[1] // count
    for k in range(count):
        at = pl.ds(k * rows, rows)
        product = dot(block, weights[k][...], 1, 1).reshape(ny, rows, out_ref.shape[2])
        if not flip:
            product = product + rest[0][:, at, :]
        out_ref[:, at, :] = product.astype(out_ref.dtype)


def activations_kernel(core_ref, gate_up_ref, back_ref, out_ref):
    rows = out_ref.shape[1]
    gate_sum = gate_up_ref[:rows, :]
    up_sum = gate_up_ref[rows:, :]
    grad_hidden = jnp.sum(back_ref[...].astype(F32), axis=0)
    sigmoid_gate = jax.nn.sigmoid(gate_sum)
    activated = gate_sum * sigmoid_gate
    out_ref[0] = (
        grad_hidden * up_sum * sigmoid_gate * (1.0 + gate_sum * (1.0 - sigmoid_gate))
    ).astype(BF16)
    out_ref[1] = (grad_hidden * activated).astype(BF16)
    out_ref[2] = (activated * up_sum).astype(BF16)


def inputs_kernel(core_ref, own_ref, other_ref, gate_ref, up_ref, out_ref):
    half = out_ref.shape[0] // 2
    for pieces, side in ((own_ref, core_ref[0]), (other_ref, 1 - core_ref[0])):
        columns = pieces.shape[-1]
        grad_gate_act = pieces[:, 0].reshape(half, columns)
        grad_up_act = pieces[:, 1].reshape(half, columns)
        share = dot(grad_gate_act, gate_ref[...], 1, 0) + dot(grad_up_act, up_ref[...], 1, 0)
        at = pl.ds(pl.multiple_of(side * half, half), half)
        out_ref[at, :] = share.astype(BF16)


def build(sizes):
    ny, nc, nz, nx = sizes

    def on_device(inputs, w_gate, w_up, w_down, cotangent):
        width, columns = w_gate.shape
        rows = inputs.shape[0]
        tokens = rows * nz * nx
        half = tokens // nc
        share_rows = half // ny
        core = lax.axis_index("c")
        gate_t, up_t = w_gate.T, w_up.T

        both = jnp.concatenate([inputs, cotangent], axis=1)
        along_z = spread(both, "z", nz).reshape(nz * rows, 2 * width)

        def add_over_cores(block, weights, out_type):
            count = len(weights)
            shape = (ny, count * share_rows, columns)
            flops = 2 * half * width * columns * count
            moved = 2 * (half * width + count * width * columns) + 4 * count * half * columns
            received = sibling(
                local(
                    functools.partial(sums_kernel, count, True),
                    jax.ShapeDtypeStruct(shape, F32),
                    flops,
                    moved,
                    core,
                    block,
                    *weights,
                )
            )
            return local(
                functools.partial(sums_kernel, count, False),
                jax.ShapeDtypeStruct(shape, out_type),
                flops,
                moved + 4 * count * half * columns,
                core,
                block,
                *weights,
                received,
            )

        all_inputs = spread(along_z[:, :width], "x", nx).reshape(tokens, width)
        chip_gate_up = add_over_cores(all_inputs, (gate_t, up_t), F32)
        gate_up = lax.psum_scatter(
            chip_gate_up.reshape(2 * half, columns), "y", scatter_dimension=0, tiled=True
        )
        all_cotangent = spread(after(along_z[:, width:], chip_gate_up), "x", nx).reshape(
            tokens, width
        )
        back = lax.all_to_all(add_over_cores(all_cotangent, (w_down,), BF16), "y", 0, 0)

        pieces = local(
            activations_kernel,
            jax.ShapeDtypeStruct((3, share_rows, columns), BF16),
            20 * share_rows * columns,
            2 * half * columns,
            core,
            gate_up,
            back,
        )
        own = lax.all_gather(pieces, "y")
        other = sibling(own[:, :2])
        share = local(
            inputs_kernel,
            jax.ShapeDtypeStruct((tokens, width), BF16),
            4 * tokens * width * columns,
            4 * tokens * columns + 2 * tokens * width,
            core,
            own,
            other,
            gate_t,
            up_t,
        )
        shares = lax.all_to_all(share.reshape(nx * nz, rows, width), ("x", "z"), 0, 0)
        grad_inputs = jnp.sum(shares.astype(F32), axis=0).astype(BF16)

        other_hidden = sibling(after(own[:, 2], share))

        def whole(mine, theirs):
            mine, theirs = mine.reshape(half, columns), theirs.reshape(half, columns)
            first = jnp.where(core == 0, mine, theirs)
            second = jnp.where(core == 0, theirs, mine)
            return jnp.concatenate([first, second], axis=0)

        grad_gate_act = whole(own[:, 0], after(other[:, 0], share))
        grad_up_act = whole(own[:, 1], after(other[:, 1], share))
        hidden = whole(own[:, 2], other_hidden)
        return (
            grad_inputs,
            dot(all_inputs, grad_gate_act, 0, 0).astype(BF16),
            dot(all_inputs, grad_up_act, 0, 0).astype(BF16),
            dot(hidden, all_cotangent, 0, 0).astype(BF16),
        )

    return on_device


def solution(mesh):
    row, col = mesh.devices.shape
    sizes = (row // 2, 2, col // 4, 4)
    fine = Mesh(mesh.devices.reshape(sizes), ("y", "c", "z", "x"))
    token_width = P(("z", "x"), ("y", "c"))
    width_hidden = P(("y", "c"), ("z", "x"))
    return jax.shard_map(
        build(sizes),
        mesh=fine,
        in_specs=(token_width, width_hidden, width_hidden, token_width, token_width),
        out_specs=(token_width, width_hidden, width_hidden, token_width),
        check_vma=False,
    )
```

```python
import jax
import jax.numpy as jnp
from jax import lax
from jax.experimental import pallas as pl
from jax.experimental.pallas import tpu as pltpu
from jax.sharding import Mesh, PartitionSpec as P

F32 = jnp.float32
BF16 = jnp.bfloat16
SWAP = [(0, 1), (1, 0)]


def dot(left, right, left_dim, right_dim):
    return lax.dot_general(
        left, right, (((left_dim,), (right_dim,)), ((), ())), preferred_element_type=F32
    )


def sibling(value):
    return lax.ppermute(value, "c", SWAP)


def spread(block, axis, size):
    copies = jnp.broadcast_to(block[None], (size, *block.shape))
    return lax.all_to_all(copies, axis, 0, 0)


def after(value, *earlier):
    return lax.optimization_barrier((value, *earlier))[0]


def local(kernel, out_shape, flops, moved, core, *operands):
    return pl.pallas_call(
        kernel,
        out_shape=out_shape,
        in_specs=[pl.BlockSpec(memory_space=pltpu.SMEM)]
        + [pl.BlockSpec(memory_space=pltpu.VMEM)] * len(operands),
        out_specs=jax.tree.map(lambda _: pl.BlockSpec(memory_space=pltpu.VMEM), out_shape),
        compiler_params=pltpu.CompilerParams(vmem_limit_bytes=24 * 1024 * 1024),
        cost_estimate=pl.CostEstimate(flops=flops, bytes_accessed=moved, transcendentals=0),
    )(core.reshape(1).astype(jnp.int32), *operands)


def sums_kernel(core_ref, block_ref, own_ref, sib_ref, own_down_ref, sib_down_ref, out_ref):
    core = core_ref[0]
    packed, width = own_ref.shape
    half = block_ref.shape[0] * block_ref.shape[2]
    own = block_ref[:, core].reshape(half, 2 * width)
    sib = block_ref[:, 1 - core].reshape(half, 2 * width)
    sums = dot(own[:, :width], own_ref[...], 1, 1) + dot(sib[:, :width], sib_ref[...], 1, 1)
    back = dot(own[:, width:], own_down_ref[...], 1, 1) + dot(
        sib[:, width:], sib_down_ref[...], 1, 1
    )
    ny, rows, _ = out_ref.shape
    out_ref[:, :, :packed] = sums.astype(BF16).reshape(ny, rows, packed)
    out_ref[:, :, packed:] = back.astype(BF16).reshape(ny, rows, packed // 2)


def activations_kernel(core_ref, parts_ref, out_ref):
    columns = parts_ref.shape[2] // 3
    sums = jnp.sum(parts_ref[...].astype(F32), axis=0)
    gate_sum = sums[:, :columns]
    up_sum = sums[:, columns : 2 * columns]
    grad_hidden = sums[:, 2 * columns :]
    sigmoid_gate = jax.nn.sigmoid(gate_sum)
    activated = gate_sum * sigmoid_gate
    out_ref[:, :columns] = (
        grad_hidden * up_sum * sigmoid_gate * (1.0 + gate_sum * (1.0 - sigmoid_gate))
    ).astype(BF16)
    out_ref[:, columns : 2 * columns] = (grad_hidden * activated).astype(BF16)
    out_ref[:, 2 * columns :] = (activated * up_sum).astype(BF16)


def share_kernel(core_ref, pieces_ref, weight_ref, out_ref):
    packed = weight_ref.shape[0]
    pieces = pieces_ref[:, :, :packed].reshape(out_ref.shape[0], packed)
    out_ref[...] = dot(pieces, weight_ref[...], 1, 0).astype(BF16)


def join_kernel(core_ref, mine_ref, theirs_ref, out_ref):
    half = mine_ref.shape[0]
    out_ref[pl.ds(pl.multiple_of(core_ref[0] * half, half), half), :] = mine_ref[...]
    out_ref[pl.ds(pl.multiple_of((1 - core_ref[0]) * half, half), half), :] = theirs_ref[...]


def weights_kernel(
    core_ref,
    own_ref,
    other_ref,
    own_block_ref,
    other_block_ref,
    gate_ref,
    up_ref,
    down_ref,
):
    columns, width = gate_ref.shape
    half = own_ref.shape[0] * own_ref.shape[1]
    core = core_ref[0]
    own = own_ref[...].reshape(half, 3 * columns)
    other = other_ref[...].reshape(half, 3 * columns)
    own_block = own_block_ref[:, core].reshape(half, 2 * width)
    other_block = other_block_ref[...].reshape(half, 2 * width)
    packed = dot(own[:, : 2 * columns], own_block[:, :width], 0, 0) + dot(
        other[:, : 2 * columns], other_block[:, :width], 0, 0
    )
    gate_ref[...] = packed[:columns].astype(BF16)
    up_ref[...] = packed[columns:].astype(BF16)
    down_ref[...] = (
        dot(own[:, 2 * columns :], own_block[:, width:], 0, 0)
        + dot(other[:, 2 * columns :], other_block[:, width:], 0, 0)
    ).astype(BF16)


def build(sizes):
    ny, nc, nh, nl, nx = sizes
    nz = nh * nl

    def on_device(inputs, w_gate, w_up, w_down, cotangent):
        width, columns = w_gate.shape
        rows = inputs.shape[0]
        part = nl * rows
        half = part * nx
        share_rows = half // ny
        core = lax.axis_index("c")
        both = jnp.concatenate([inputs, cotangent], axis=1)
        along_z = lax.all_gather(both, ("h", "l", "c"), axis=0, tiled=True)
        along_z = along_z.reshape(nh, nl, nc, rows, 2 * width)
        kept = lax.dynamic_index_in_dim(along_z, core, 0, False)
        kept = kept.swapaxes(0, 1).reshape(nc, part, 2 * width)

        w_gate, w_up, w_down = (after(w, along_z) for w in (w_gate, w_up, w_down))
        own_gate_up = jnp.concatenate([w_gate.T, w_up.T], axis=0)
        sib_gate_up, sib_down = sibling(own_gate_up), sibling(w_down)
        block = spread(kept, "x", nx)
        sums = local(
            sums_kernel,
            jax.ShapeDtypeStruct((ny, share_rows, 3 * columns), BF16),
            12 * half * width * columns,
            8 * half * width + 12 * columns * width + 6 * half * columns,
            core,
            block,
            own_gate_up,
            sib_gate_up,
            w_down,
            sib_down,
        )
        pieces = local(
            activations_kernel,
            jax.ShapeDtypeStruct((share_rows, 3 * columns), BF16),
            20 * share_rows * columns,
            6 * half * columns,
            core,
            lax.all_to_all(sums, "y", 0, 0),
        )
        pieces = lax.all_gather(pieces, "y")

        def share(weight):
            return local(
                share_kernel,
                jax.ShapeDtypeStruct((half, width), BF16),
                4 * half * width * columns,
                6 * half * columns + 2 * half * width + 4 * columns * width,
                core,
                pieces,
                weight,
            )

        theirs = sibling(share(sib_gate_up))
        mine = share(own_gate_up)
        shares = local(
            join_kernel,
            jax.ShapeDtypeStruct((2 * half, width), BF16),
            0,
            8 * half * width,
            core,
            mine,
            theirs,
        )
        parts = lax.all_to_all(
            shares.reshape(nz * nx, rows, width), ("h", "x", "l"), 0, 0
        )
        grad_inputs = jnp.sum(parts.astype(F32), axis=0).astype(BF16)

        gradient = jax.ShapeDtypeStruct((columns, width), BF16)
        grad_gate, grad_up, grad_down = local(
            weights_kernel,
            (gradient, gradient, gradient),
            12 * half * width * columns,
            12 * half * columns + 8 * half * width + 6 * columns * width,
            core,
            pieces,
            sibling(after(pieces, shares)),
            block,
            sibling(lax.dynamic_index_in_dim(after(block, shares), 1 - core, 1, False)),
        )
        return grad_inputs, grad_gate.T, grad_up.T, grad_down

    return on_device


def solution(mesh):
    row, col = mesh.devices.shape
    sizes = (row // 2, 2, 2, col // 8, 4)
    fine = Mesh(mesh.devices.reshape(sizes), ("y", "c", "h", "l", "x"))
    token_width = P(("h", "l", "x"), ("y", "c"))
    width_hidden = P(("y", "c"), ("h", "l", "x"))
    return jax.shard_map(
        build(sizes),
        mesh=fine,
        in_specs=(token_width, width_hidden, width_hidden, token_width, token_width),
        out_specs=(token_width, width_hidden, width_hidden, token_width),
        check_vma=False,
    )
```

```python
import jax
import jax.numpy as jnp
from jax import lax
from jax.experimental import pallas as pl
from jax.experimental.pallas import tpu as pltpu
from jax.sharding import Mesh, PartitionSpec as P

F32 = jnp.float32
BF16 = jnp.bfloat16
SWAP = [(0, 1), (1, 0)]


def dot(left, right, left_dim, right_dim):
    return lax.dot_general(
        left, right, (((left_dim,), (right_dim,)), ((), ())), preferred_element_type=F32
    )


def sibling(value):
    return lax.ppermute(value, "c", SWAP)


def after(value, *earlier):
    return lax.optimization_barrier((value, *earlier))[0]


def local(kernel, out_shape, flops, moved, core, *operands):
    return pl.pallas_call(
        kernel,
        out_shape=out_shape,
        in_specs=[pl.BlockSpec(memory_space=pltpu.SMEM)]
        + [pl.BlockSpec(memory_space=pltpu.VMEM)] * len(operands),
        out_specs=jax.tree.map(lambda _: pl.BlockSpec(memory_space=pltpu.VMEM), out_shape),
        compiler_params=pltpu.CompilerParams(vmem_limit_bytes=16 * 1024 * 1024),
        cost_estimate=pl.CostEstimate(flops=flops, bytes_accessed=moved, transcendentals=0),
    )(core.reshape(1).astype(jnp.int32), *operands)


def sums_kernel(core_ref, block_ref, own_ref, sib_ref, out_ref):
    core = core_ref[0]
    half = block_ref.shape[0] * block_ref.shape[2]
    own = block_ref[:, core].reshape(half, block_ref.shape[3])
    sib = block_ref[:, 1 - core].reshape(half, block_ref.shape[3])
    sums = dot(own, own_ref[...], 1, 1) + dot(sib, sib_ref[...], 1, 1)
    out_ref[...] = sums.astype(BF16).reshape(out_ref.shape)


def activations_kernel(core_ref, gate_up_ref, back_ref, out_ref, hidden_ref):
    columns = back_ref.shape[2]
    gate_up = jnp.sum(gate_up_ref[...].astype(F32), axis=0)
    gate_sum = gate_up[:, :columns]
    up_sum = gate_up[:, columns:]
    grad_hidden = jnp.sum(back_ref[...].astype(F32), axis=0)
    sigmoid_gate = jax.nn.sigmoid(gate_sum)
    activated = gate_sum * sigmoid_gate
    grad_gate_act = grad_hidden * up_sum * sigmoid_gate * (1.0 + gate_sum * (1.0 - sigmoid_gate))
    out_ref[0, :, :columns] = grad_gate_act.astype(BF16)
    out_ref[0, :, columns:] = (grad_hidden * activated).astype(BF16)
    for k in range(1, out_ref.shape[0]):
        out_ref[k] = out_ref[0]
    hidden_ref[...] = (activated * up_sum).astype(BF16)


def share_kernel(core_ref, pieces_ref, weight_ref, out_ref):
    pieces = pieces_ref[...].reshape(out_ref.shape[0], weight_ref.shape[0])
    out_ref[...] = dot(pieces, weight_ref[...], 1, 0).astype(BF16)


def shares_kernel(core_ref, mine_ref, pieces_ref, weight_ref, out_ref):
    half = mine_ref.shape[0]
    pieces = pieces_ref[...].reshape(half, weight_ref.shape[0])
    theirs = dot(pieces, weight_ref[...], 1, 0).astype(BF16)
    out_ref[pl.ds(pl.multiple_of(core_ref[0] * half, half), half), :] = mine_ref[...]
    out_ref[pl.ds(pl.multiple_of((1 - core_ref[0]) * half, half), half), :] = theirs


def weights_kernel(
    core_ref,
    own_ref,
    other_ref,
    hidden_ref,
    own_inputs_ref,
    other_inputs_ref,
    own_cotangent_ref,
    other_cotangent_ref,
    gate_ref,
    up_ref,
    down_ref,
):
    columns, width = gate_ref.shape
    half = own_ref.shape[0] * own_ref.shape[1]
    core = core_ref[0]
    own = own_ref[...].reshape(half, 2 * columns)
    other = other_ref[...].reshape(half, 2 * columns)
    own_hidden = hidden_ref[:, core].reshape(half, columns)
    other_hidden = hidden_ref[:, 1 - core].reshape(half, columns)
    own_inputs = own_inputs_ref[:, core].reshape(half, width)
    other_inputs = other_inputs_ref[...].reshape(half, width)
    own_cotangent = own_cotangent_ref[:, core].reshape(half, width)
    other_cotangent = other_cotangent_ref[...].reshape(half, width)
    packed = dot(own, own_inputs, 0, 0) + dot(other, other_inputs, 0, 0)
    gate_ref[...] = packed[:columns].astype(BF16)
    up_ref[...] = packed[columns:].astype(BF16)
    down_ref[...] = (
        dot(own_hidden, own_cotangent, 0, 0)
        + dot(other_hidden, other_cotangent, 0, 0)
    ).astype(BF16)


def total_kernel(core_ref, parts_ref, out_ref):
    out_ref[...] = jnp.sum(parts_ref[...].astype(F32), axis=0).astype(BF16)


def build(sizes):
    ny, nc, nh, nl, nx = sizes
    nz = nh * nl

    def on_device(inputs, w_gate, w_up, w_down, cotangent):
        width, columns = w_gate.shape
        rows = inputs.shape[0]
        part = nl * rows
        half = part * nx
        share_rows = half // ny
        core = lax.axis_index("c")
        both = jnp.concatenate([inputs, cotangent], axis=1)
        along_z = lax.all_gather(both, ("h", "l", "c"), axis=0, tiled=True)
        along_z = along_z.reshape(nh, nl, nc, rows, 2 * width)
        kept = lax.dynamic_index_in_dim(along_z, core, 0, False)
        kept = kept.swapaxes(0, 1).reshape(nc, part, 2 * width)

        w_gate, w_up, w_down = (after(w, along_z) for w in (w_gate, w_up, w_down))
        own_gate_up = jnp.concatenate([w_gate.T, w_up.T], axis=0)
        sib_gate_up, sib_down = sibling(own_gate_up), sibling(w_down)
        def sums(block, own, sib):
            return local(
                sums_kernel,
                jax.ShapeDtypeStruct((ny, share_rows, own.shape[0]), BF16),
                4 * half * width * own.shape[0],
                4 * (half + own.shape[0]) * width + 2 * half * own.shape[0],
                core,
                block,
                own,
                sib,
            )

        def of_other_tokens(block, earlier):
            return sibling(lax.dynamic_index_in_dim(after(block, earlier), 1 - core, 1, False))

        all_inputs = lax.all_gather(kept[:, :, :width], "x")
        gate_up = sums(all_inputs, own_gate_up, sib_gate_up)
        all_cotangent = lax.all_gather(after(kept[:, :, width:], gate_up), "x")
        other_inputs = of_other_tokens(all_inputs, gate_up)
        gate_up = lax.all_to_all(gate_up, "y", 0, 0)
        back = sums(after(all_cotangent, gate_up, other_inputs), w_down, sib_down)
        back = lax.all_to_all(back, "y", 0, 0)
        pieces, hidden = local(
            activations_kernel,
            (
                jax.ShapeDtypeStruct((ny, share_rows, 2 * columns), BF16),
                jax.ShapeDtypeStruct((share_rows, columns), BF16),
            ),
            20 * share_rows * columns,
            10 * half * columns,
            core,
            gate_up,
            back,
        )
        pieces = lax.all_to_all(pieces, "y", 0, 0)

        other_pieces = sibling(pieces)
        flops = 4 * half * width * columns
        moved = 4 * half * columns + 2 * half * width + 4 * columns * width
        mine = local(
            share_kernel,
            jax.ShapeDtypeStruct((half, width), BF16),
            flops,
            moved,
            core,
            pieces,
            own_gate_up,
        )
        shares = local(
            shares_kernel,
            pltpu.HBM((2 * half, width), BF16),
            flops,
            moved + 4 * half * width,
            core,
            mine,
            other_pieces,
            own_gate_up,
        )
        parts = lax.all_to_all(
            shares.reshape(nz * nx, rows, width), ("h", "x", "l"), 0, 0
        )
        grad_inputs = local(
            total_kernel,
            jax.ShapeDtypeStruct((rows, width), BF16),
            2 * half * width,
            4 * half * width,
            core,
            parts,
        )

        gradient = jax.ShapeDtypeStruct((columns, width), BF16)
        grad_gate, grad_up, grad_down = local(
            weights_kernel,
            (gradient, gradient, gradient),
            12 * half * width * columns,
            12 * half * columns + 8 * half * width + 6 * columns * width,
            core,
            pieces,
            other_pieces,
            lax.all_gather(after(hidden, shares), ("y", "c"), axis=0, tiled=True).reshape(
                ny, nc, share_rows, columns
            ),
            all_inputs,
            other_inputs,
            all_cotangent,
            of_other_tokens(all_cotangent, shares),
        )
        return grad_inputs, grad_gate.T, grad_up.T, grad_down

    return on_device


def solution(mesh):
    row, col = mesh.devices.shape
    sizes = (row // 2, 2, 2, col // 8, 4)
    fine = Mesh(mesh.devices.reshape(sizes), ("y", "c", "h", "l", "x"))
    token_width = P(("h", "l", "x"), ("y", "c"))
    width_hidden = P(("y", "c"), ("h", "l", "x"))
    return jax.shard_map(
        build(sizes),
        mesh=fine,
        in_specs=(token_width, width_hidden, width_hidden, token_width, token_width),
        out_specs=(token_width, width_hidden, width_hidden, token_width),
        check_vma=False,
    )
```

```python
import jax
import jax.numpy as jnp
from jax import lax
from jax.experimental import pallas as pl
from jax.experimental.pallas import tpu as pltpu
from jax.sharding import Mesh, PartitionSpec as P

F32 = jnp.float32
BF16 = jnp.bfloat16
SWAP = [(0, 1), (1, 0)]


def dot(left, right, left_dim, right_dim):
    return lax.dot_general(
        left, right, (((left_dim,), (right_dim,)), ((), ())), preferred_element_type=F32
    )


def sibling(value):
    return lax.ppermute(value, "c", SWAP)


def after(value, *earlier):
    return lax.optimization_barrier((value, *earlier))[0]


def local(kernel, out_shape, flops, moved, core, *operands, fetched=()):
    scratch = [pltpu.VMEM(value.shape, value.dtype) for value in fetched]
    if fetched:
        scratch.append(pltpu.SemaphoreType.DMA((len(fetched),)))
    spaces = [pltpu.SMEM] + [pltpu.VMEM] * len(operands) + [pltpu.HBM] * len(fetched)
    return pl.pallas_call(
        kernel,
        out_shape=out_shape,
        in_specs=[pl.BlockSpec(memory_space=space) for space in spaces],
        out_specs=jax.tree.map(lambda _: pl.BlockSpec(memory_space=pltpu.VMEM), out_shape),
        scratch_shapes=scratch,
        compiler_params=pltpu.CompilerParams(vmem_limit_bytes=16 * 1024 * 1024),
        cost_estimate=pl.CostEstimate(flops=flops, bytes_accessed=moved, transcendentals=0),
    )(
        core.reshape(1).astype(jnp.int32),
        *operands,
        *(pltpu.with_memory_space_constraint(value, pltpu.HBM) for value in fetched),
    )


def sums_kernel(
    core_ref,
    block_ref,
    own_ref,
    sib_ref,
    own_down_hbm,
    sib_down_hbm,
    out_ref,
    own_down_ref,
    sib_down_ref,
    semaphores,
):
    own_copy = pltpu.make_async_copy(own_down_hbm, own_down_ref, semaphores.at[0])
    sib_copy = pltpu.make_async_copy(sib_down_hbm, sib_down_ref, semaphores.at[1])
    own_copy.start()
    sib_copy.start()
    core = core_ref[0]
    packed, width = own_ref.shape
    half = block_ref.shape[0] * block_ref.shape[2]
    own = block_ref[:, core].reshape(half, 2 * width)
    sib = block_ref[:, 1 - core].reshape(half, 2 * width)
    ny, rows, _ = out_ref.shape
    sums = dot(own[:, :width], own_ref[...], 1, 1) + dot(sib[:, :width], sib_ref[...], 1, 1)
    out_ref[:, :, :packed] = sums.astype(BF16).reshape(ny, rows, packed)
    own_copy.wait()
    sib_copy.wait()
    back = dot(own[:, width:], own_down_ref[...], 1, 1) + dot(
        sib[:, width:], sib_down_ref[...], 1, 1
    )
    out_ref[:, :, packed:] = back.astype(BF16).reshape(ny, rows, packed // 2)


def activations_kernel(core_ref, parts_ref, out_ref, hidden_ref):
    columns = hidden_ref.shape[1]
    sums = jnp.sum(parts_ref[...].astype(F32), axis=0)
    gate_sum = sums[:, :columns]
    up_sum = sums[:, columns : 2 * columns]
    grad_hidden = sums[:, 2 * columns :]
    sigmoid_gate = jax.nn.sigmoid(gate_sum)
    activated = gate_sum * sigmoid_gate
    grad_gate_act = grad_hidden * up_sum * sigmoid_gate * (1.0 + gate_sum * (1.0 - sigmoid_gate))
    out_ref[0, :, :columns] = grad_gate_act.astype(BF16)
    out_ref[0, :, columns:] = (grad_hidden * activated).astype(BF16)
    for k in range(1, out_ref.shape[0]):
        out_ref[k] = out_ref[0]
    hidden_ref[...] = (activated * up_sum).astype(BF16)


def share_kernel(core_ref, pieces_ref, weight_ref, out_ref):
    packed = pieces_ref.shape[2]
    pieces = pieces_ref[...].reshape(out_ref.shape[0], packed)
    out_ref[...] = dot(pieces, weight_ref[...], 1, 0).astype(BF16)


def shares_kernel(core_ref, mine_ref, pieces_ref, weight_ref, out_ref):
    half = mine_ref.shape[0]
    packed = pieces_ref.shape[2]
    pieces = pieces_ref[...].reshape(half, packed)
    theirs = dot(pieces, weight_ref[...], 1, 0).astype(BF16)
    out_ref[pl.ds(pl.multiple_of(core_ref[0] * half, half), half), :] = mine_ref[...]
    out_ref[pl.ds(pl.multiple_of((1 - core_ref[0]) * half, half), half), :] = theirs


def weights_kernel(
    core_ref,
    own_ref,
    other_ref,
    hidden_ref,
    own_block_ref,
    other_block_ref,
    gate_ref,
    up_ref,
    down_ref,
):
    columns, width = gate_ref.shape
    half = own_ref.shape[0] * own_ref.shape[1]
    core = core_ref[0]
    own = own_ref[...].reshape(half, 2 * columns)
    other = other_ref[...].reshape(half, 2 * columns)
    own_hidden = hidden_ref[:, core].reshape(half, columns)
    other_hidden = hidden_ref[:, 1 - core].reshape(half, columns)
    own_block = own_block_ref[:, core].reshape(half, 2 * width)
    own_inputs, own_cotangent = own_block[:, :width], own_block[:, width:]
    other_block = other_block_ref[...].reshape(half, 2 * width)
    other_inputs, other_cotangent = other_block[:, :width], other_block[:, width:]
    packed = dot(own, own_inputs, 0, 0) + dot(other, other_inputs, 0, 0)
    gate_ref[...] = packed[:columns].astype(BF16)
    up_ref[...] = packed[columns:].astype(BF16)
    down_ref[...] = (
        dot(own_hidden, own_cotangent, 0, 0)
        + dot(other_hidden, other_cotangent, 0, 0)
    ).astype(BF16)


def total_kernel(core_ref, parts_ref, out_ref):
    out_ref[...] = jnp.sum(parts_ref[...].astype(F32), axis=0).astype(BF16)


def build(sizes):
    ny, nc, nh, nl, nx = sizes
    nz = nh * nl

    def on_device(inputs, w_gate, w_up, w_down, cotangent):
        width, columns = w_gate.shape
        rows = inputs.shape[0]
        part = nl * rows
        half = part * nx
        share_rows = half // ny
        core = lax.axis_index("c")
        both = jnp.concatenate([inputs, cotangent], axis=1)
        along_z = lax.all_gather(both, ("h", "l", "c"), axis=0, tiled=True)
        along_z = along_z.reshape(nh, nl, nc, rows, 2 * width)
        kept = lax.dynamic_index_in_dim(along_z, core, 0, False)
        kept = kept.swapaxes(0, 1).reshape(nc, part, 2 * width)

        w_gate, w_up, w_down = (after(w, along_z) for w in (w_gate, w_up, w_down))
        own_gate_up = jnp.concatenate([w_gate.T, w_up.T], axis=0)
        sib_gate_up, sib_down = sibling(own_gate_up), sibling(w_down)
        block = lax.all_to_all(jnp.broadcast_to(kept[None], (nx, *kept.shape)), "x", 0, 0)
        sums = local(
            sums_kernel,
            jax.ShapeDtypeStruct((ny, share_rows, 3 * columns), BF16),
            12 * half * width * columns,
            8 * half * width + 12 * columns * width + 6 * half * columns,
            core,
            block,
            own_gate_up,
            sib_gate_up,
            fetched=(w_down, sib_down),
        )
        sums = lax.all_to_all(sums, "y", 0, 0)
        pieces, hidden = local(
            activations_kernel,
            (
                jax.ShapeDtypeStruct((ny, share_rows, 2 * columns), BF16),
                jax.ShapeDtypeStruct((share_rows, columns), BF16),
            ),
            20 * share_rows * columns,
            10 * half * columns,
            core,
            sums,
        )
        pieces = lax.all_to_all(pieces, "y", 0, 0)

        other_pieces = sibling(pieces)
        flops = 4 * half * width * columns
        moved = 4 * half * columns + 2 * half * width + 4 * columns * width
        mine = local(
            share_kernel,
            jax.ShapeDtypeStruct((half, width), BF16),
            flops,
            moved,
            core,
            pieces,
            own_gate_up,
        )
        shares = local(
            shares_kernel,
            pltpu.HBM((2 * half, width), BF16),
            flops,
            moved + 4 * half * width,
            core,
            mine,
            other_pieces,
            own_gate_up,
        )
        parts = lax.all_to_all(
            shares.reshape(nz * nx, rows, width), ("h", "x", "l"), 0, 0
        )
        grad_inputs = local(
            total_kernel,
            jax.ShapeDtypeStruct((rows, width), BF16),
            2 * half * width,
            4 * half * width,
            core,
            parts,
        )

        gradient = jax.ShapeDtypeStruct((columns, width), BF16)
        grad_gate, grad_up, grad_down = local(
            weights_kernel,
            (gradient, gradient, gradient),
            12 * half * width * columns,
            12 * half * columns + 8 * half * width + 6 * columns * width,
            core,
            pieces,
            other_pieces,
            lax.all_gather(after(hidden, shares), ("y", "c"), axis=0, tiled=True).reshape(
                ny, nc, share_rows, columns
            ),
            block,
            sibling(lax.dynamic_index_in_dim(after(block, shares), 1 - core, 1, False)),
        )
        return grad_inputs, grad_gate.T, grad_up.T, grad_down

    return on_device


def solution(mesh):
    row, col = mesh.devices.shape
    sizes = (row // 2, 2, 2, col // 8, 4)
    fine = Mesh(mesh.devices.reshape(sizes), ("y", "c", "h", "l", "x"))
    token_width = P(("h", "l", "x"), ("y", "c"))
    width_hidden = P(("y", "c"), ("h", "l", "x"))
    return jax.shard_map(
        build(sizes),
        mesh=fine,
        in_specs=(token_width, width_hidden, width_hidden, token_width, token_width),
        out_specs=(token_width, width_hidden, width_hidden, token_width),
        check_vma=False,
    )
```

```python
import jax
import jax.numpy as jnp
from jax import lax
from jax.experimental import pallas as pl
from jax.experimental.pallas import tpu as pltpu
from jax.sharding import Mesh, PartitionSpec as P

F32 = jnp.float32
BF16 = jnp.bfloat16
SWAP = [(0, 1), (1, 0)]


def dot(left, right, left_dim, right_dim):
    return lax.dot_general(
        left, right, (((left_dim,), (right_dim,)), ((), ())), preferred_element_type=F32
    )


def sibling(value):
    return lax.ppermute(value, "c", SWAP)


def after(value, *earlier):
    return lax.optimization_barrier((value, *earlier))[0]


def local(kernel, out_shape, flops, moved, core, *operands, fetched=()):
    scratch = [pltpu.VMEM(value.shape, value.dtype) for value in fetched]
    if fetched:
        scratch.append(pltpu.SemaphoreType.DMA((len(fetched),)))
    spaces = [pltpu.SMEM] + [pltpu.VMEM] * len(operands) + [pltpu.HBM] * len(fetched)
    return pl.pallas_call(
        kernel,
        out_shape=out_shape,
        in_specs=[pl.BlockSpec(memory_space=space) for space in spaces],
        out_specs=jax.tree.map(lambda _: pl.BlockSpec(memory_space=pltpu.VMEM), out_shape),
        scratch_shapes=scratch,
        compiler_params=pltpu.CompilerParams(vmem_limit_bytes=16 * 1024 * 1024),
        cost_estimate=pl.CostEstimate(flops=flops, bytes_accessed=moved, transcendentals=0),
    )(
        core.reshape(1).astype(jnp.int32),
        *operands,
        *(pltpu.with_memory_space_constraint(value, pltpu.HBM) for value in fetched),
    )


def sums_kernel(
    core_ref,
    block_ref,
    own_ref,
    sib_ref,
    own_down_hbm,
    sib_down_hbm,
    out_ref,
    own_down_ref,
    sib_down_ref,
    semaphores,
):
    own_copy = pltpu.make_async_copy(own_down_hbm, own_down_ref, semaphores.at[0])
    sib_copy = pltpu.make_async_copy(sib_down_hbm, sib_down_ref, semaphores.at[1])
    own_copy.start()
    sib_copy.start()
    core = core_ref[0]
    packed, width = own_ref.shape
    half = block_ref.shape[0] * block_ref.shape[2]
    own = block_ref[:, core].reshape(half, 2 * width)
    sib = block_ref[:, 1 - core].reshape(half, 2 * width)
    ny, rows, _ = out_ref.shape

    def store(sums, start):
        count = sums.shape[1]
        pairs = sums.reshape(ny, 2 * rows, count)
        out_ref[:, :, start : start + count] = pairs[:, :rows].astype(BF16)
        out_ref[:, :, start + count : start + 2 * count] = pairs[:, rows:].astype(BF16)

    store(dot(own[:, :width], own_ref[...], 1, 1) + dot(sib[:, :width], sib_ref[...], 1, 1), 0)
    own_copy.wait()
    sib_copy.wait()
    back = dot(own[:, width:], own_down_ref[...], 1, 1)
    store(back + dot(sib[:, width:], sib_down_ref[...], 1, 1), 2 * packed)


def activations_kernel(core_ref, parts_ref, out_ref, hidden_ref):
    columns = hidden_ref.shape[1]
    sums = jnp.sum(parts_ref[...].astype(F32), axis=0)
    gate_up = jnp.concatenate([sums[:, : 2 * columns], sums[:, 2 * columns : 4 * columns]], axis=0)
    gate_sum = gate_up[:, :columns]
    up_sum = gate_up[:, columns:]
    grad_hidden = jnp.concatenate(
        [sums[:, 4 * columns : 5 * columns], sums[:, 5 * columns :]], axis=0
    )
    sigmoid_gate = jax.nn.sigmoid(gate_sum)
    activated = gate_sum * sigmoid_gate
    grad_gate_act = grad_hidden * up_sum * sigmoid_gate * (1.0 + gate_sum * (1.0 - sigmoid_gate))
    out_ref[0, :, :columns] = grad_gate_act.astype(BF16)
    out_ref[0, :, columns:] = (grad_hidden * activated).astype(BF16)
    for k in range(1, out_ref.shape[0]):
        out_ref[k] = out_ref[0]
    hidden_ref[...] = (activated * up_sum).astype(BF16)


def share_kernel(core_ref, pieces_ref, weight_ref, out_ref):
    packed = pieces_ref.shape[2]
    pieces = pieces_ref[...].reshape(out_ref.shape[0], packed)
    out_ref[...] = dot(pieces, weight_ref[...], 1, 0).astype(BF16)


def shares_kernel(core_ref, mine_ref, pieces_ref, weight_ref, out_ref):
    half = mine_ref.shape[0]
    packed = pieces_ref.shape[2]
    pieces = pieces_ref[...].reshape(half, packed)
    theirs = dot(pieces, weight_ref[...], 1, 0).astype(BF16)
    out_ref[pl.ds(pl.multiple_of(core_ref[0] * half, half), half), :] = mine_ref[...]
    out_ref[pl.ds(pl.multiple_of((1 - core_ref[0]) * half, half), half), :] = theirs


def weights_kernel(
    core_ref,
    own_ref,
    other_ref,
    hidden_ref,
    own_block_ref,
    other_block_ref,
    gate_ref,
    up_ref,
    down_ref,
):
    columns, width = gate_ref.shape
    half = own_ref.shape[0] * own_ref.shape[1]
    core = core_ref[0]
    own = own_ref[...].reshape(half, 2 * columns)
    other = other_ref[...].reshape(half, 2 * columns)
    own_hidden = hidden_ref[:, core].reshape(half, columns)
    other_hidden = hidden_ref[:, 1 - core].reshape(half, columns)
    own_block = own_block_ref[:, core].reshape(half, 2 * width)
    own_inputs, own_cotangent = own_block[:, :width], own_block[:, width:]
    other_block = other_block_ref[...].reshape(half, 2 * width)
    other_inputs, other_cotangent = other_block[:, :width], other_block[:, width:]
    packed = dot(own, own_inputs, 0, 0) + dot(other, other_inputs, 0, 0)
    gate_ref[...] = packed[:columns].astype(BF16)
    up_ref[...] = packed[columns:].astype(BF16)
    down_ref[...] = (
        dot(own_hidden, own_cotangent, 0, 0)
        + dot(other_hidden, other_cotangent, 0, 0)
    ).astype(BF16)


def total_kernel(core_ref, parts_ref, out_ref):
    out_ref[...] = jnp.sum(parts_ref[...].astype(F32), axis=0).astype(BF16)


def build(sizes):
    ny, nc, nh, nl, nx = sizes
    nz = nh * nl

    def on_device(inputs, w_gate, w_up, w_down, cotangent):
        width, columns = w_gate.shape
        rows = inputs.shape[0]
        part = nl * rows
        half = part * nx
        share_rows = half // ny
        core = lax.axis_index("c")
        both = jnp.concatenate([inputs, cotangent], axis=1)
        along_z = lax.all_gather(both, ("h", "l", "c"), axis=0, tiled=True)
        along_z = along_z.reshape(nh, nl, nc, rows, 2 * width)
        kept = lax.dynamic_index_in_dim(along_z, core, 0, False)
        kept = kept.swapaxes(0, 1).reshape(nc, part, 2 * width)

        w_gate, w_up, w_down = (after(w, along_z) for w in (w_gate, w_up, w_down))
        own_gate_up = jnp.concatenate([w_gate.T, w_up.T], axis=0)
        sib_gate_up, sib_down = sibling(own_gate_up), sibling(w_down)
        block = lax.all_to_all(jnp.broadcast_to(kept[None], (nx, *kept.shape)), "x", 0, 0)
        sums = local(
            sums_kernel,
            jax.ShapeDtypeStruct((ny, share_rows // 2, 6 * columns), BF16),
            12 * half * width * columns,
            8 * half * width + 12 * columns * width + 6 * half * columns,
            core,
            block,
            own_gate_up,
            sib_gate_up,
            fetched=(w_down, sib_down),
        )
        sums = lax.all_to_all(sums, "y", 0, 0)
        pieces, hidden = local(
            activations_kernel,
            (
                jax.ShapeDtypeStruct((ny, share_rows, 2 * columns), BF16),
                jax.ShapeDtypeStruct((share_rows, columns), BF16),
            ),
            20 * share_rows * columns,
            10 * half * columns,
            core,
            sums,
        )
        pieces = lax.all_to_all(pieces, "y", 0, 0)

        other_pieces = sibling(pieces)
        flops = 4 * half * width * columns
        moved = 4 * half * columns + 2 * half * width + 4 * columns * width
        mine = local(
            share_kernel,
            jax.ShapeDtypeStruct((half, width), BF16),
            flops,
            moved,
            core,
            pieces,
            own_gate_up,
        )
        shares = local(
            shares_kernel,
            pltpu.HBM((2 * half, width), BF16),
            flops,
            moved + 4 * half * width,
            core,
            mine,
            other_pieces,
            own_gate_up,
        )
        parts = lax.all_to_all(
            shares.reshape(nz * nx, rows, width), ("h", "x", "l"), 0, 0
        )
        grad_inputs = local(
            total_kernel,
            jax.ShapeDtypeStruct((rows, width), BF16),
            2 * half * width,
            4 * half * width,
            core,
            parts,
        )

        gradient = jax.ShapeDtypeStruct((columns, width), BF16)
        grad_gate, grad_up, grad_down = local(
            weights_kernel,
            (gradient, gradient, gradient),
            12 * half * width * columns,
            12 * half * columns + 8 * half * width + 6 * columns * width,
            core,
            pieces,
            other_pieces,
            lax.all_gather(after(hidden, shares), ("y", "c"), axis=0, tiled=True).reshape(
                ny, nc, share_rows, columns
            ),
            block,
            sibling(lax.dynamic_index_in_dim(after(block, shares), 1 - core, 1, False)),
        )
        return grad_inputs, grad_gate.T, grad_up.T, grad_down

    return on_device


def solution(mesh):
    row, col = mesh.devices.shape
    sizes = (row // 2, 2, 2, col // 8, 4)
    fine = Mesh(mesh.devices.reshape(sizes), ("y", "c", "h", "l", "x"))
    token_width = P(("h", "l", "x"), ("y", "c"))
    width_hidden = P(("y", "c"), ("h", "l", "x"))
    return jax.shard_map(
        build(sizes),
        mesh=fine,
        in_specs=(token_width, width_hidden, width_hidden, token_width, token_width),
        out_specs=(token_width, width_hidden, width_hidden, token_width),
        check_vma=False,
    )
```

```python
import jax
import jax.numpy as jnp
from jax import lax
from jax.experimental import pallas as pl
from jax.experimental.pallas import tpu as pltpu
from jax.sharding import Mesh, PartitionSpec as P

F32 = jnp.float32
BF16 = jnp.bfloat16
SWAP = [(0, 1), (1, 0)]


def dot(left, right, left_dim, right_dim):
    return lax.dot_general(
        left, right, (((left_dim,), (right_dim,)), ((), ())), preferred_element_type=F32
    )


def sibling(value):
    return lax.ppermute(value, "c", SWAP)


def after(value, *earlier):
    return lax.optimization_barrier((value, *earlier))[0]


def local(kernel, out_shape, flops, moved, core, *operands, fetched=()):
    scratch = [pltpu.VMEM(value.shape, value.dtype) for value in fetched]
    if fetched:
        scratch.append(pltpu.SemaphoreType.DMA((len(fetched),)))
    spaces = [pltpu.SMEM] + [pltpu.VMEM] * len(operands) + [pltpu.HBM] * len(fetched)
    return pl.pallas_call(
        kernel,
        out_shape=out_shape,
        in_specs=[pl.BlockSpec(memory_space=space) for space in spaces],
        out_specs=jax.tree.map(lambda _: pl.BlockSpec(memory_space=pltpu.VMEM), out_shape),
        scratch_shapes=scratch,
        compiler_params=pltpu.CompilerParams(vmem_limit_bytes=16 * 1024 * 1024),
        cost_estimate=pl.CostEstimate(flops=flops, bytes_accessed=moved, transcendentals=0),
    )(
        core.reshape(1).astype(jnp.int32),
        *operands,
        *(pltpu.with_memory_space_constraint(value, pltpu.HBM) for value in fetched),
    )


def sums_kernel(
    core_ref,
    block_ref,
    own_ref,
    sib_ref,
    own_down_hbm,
    sib_down_hbm,
    out_ref,
    own_down_ref,
    sib_down_ref,
    semaphores,
):
    own_copy = pltpu.make_async_copy(own_down_hbm, own_down_ref, semaphores.at[0])
    sib_copy = pltpu.make_async_copy(sib_down_hbm, sib_down_ref, semaphores.at[1])
    own_copy.start()
    sib_copy.start()
    core = core_ref[0]
    packed, width = own_ref.shape
    half = block_ref.shape[0] * block_ref.shape[2]
    own = block_ref[:, core].reshape(half, 2 * width)
    sib = block_ref[:, 1 - core].reshape(half, 2 * width)
    ny, rows, _ = out_ref.shape

    def store(sums, start):
        count = sums.shape[1]
        pairs = sums.reshape(ny, 2 * rows, count)
        out_ref[:, :, start : start + count] = pairs[:, :rows].astype(BF16)
        out_ref[:, :, start + count : start + 2 * count] = pairs[:, rows:].astype(BF16)

    store(dot(own[:, :width], own_ref[...], 1, 1) + dot(sib[:, :width], sib_ref[...], 1, 1), 0)
    own_copy.wait()
    sib_copy.wait()
    back = dot(own[:, width:], own_down_ref[...], 1, 1)
    store(back + dot(sib[:, width:], sib_down_ref[...], 1, 1), 2 * packed)


def sigmoid(value):
    small = jnp.exp(-jnp.abs(value))
    return jnp.where(value >= 0.0, 1.0, small) / (1.0 + small)


def activations_kernel(core_ref, parts_ref, out_ref, hidden_ref):
    columns = hidden_ref.shape[1]
    sums = jnp.sum(parts_ref[...].astype(F32), axis=0)
    gate_up = jnp.concatenate([sums[:, : 2 * columns], sums[:, 2 * columns : 4 * columns]], axis=0)
    gate_sum = gate_up[:, :columns]
    up_sum = gate_up[:, columns:]
    grad_hidden = jnp.concatenate(
        [sums[:, 4 * columns : 5 * columns], sums[:, 5 * columns :]], axis=0
    )
    sigmoid_gate = sigmoid(gate_sum)
    activated = gate_sum * sigmoid_gate
    grad_gate_act = grad_hidden * up_sum * sigmoid_gate * (1.0 + gate_sum * (1.0 - sigmoid_gate))
    out_ref[0, :, :columns] = grad_gate_act.astype(BF16)
    out_ref[0, :, columns:] = (grad_hidden * activated).astype(BF16)
    for k in range(1, out_ref.shape[0]):
        out_ref[k] = out_ref[0]
    hidden_ref[...] = (activated * up_sum).astype(BF16)


def share_kernel(core_ref, pieces_ref, weight_ref, out_ref):
    packed = pieces_ref.shape[2]
    pieces = pieces_ref[...].reshape(out_ref.shape[0], packed)
    out_ref[...] = dot(pieces, weight_ref[...], 1, 0).astype(BF16)


def shares_kernel(core_ref, mine_ref, pieces_ref, weight_ref, out_ref):
    half = mine_ref.shape[0]
    packed = pieces_ref.shape[2]
    pieces = pieces_ref[...].reshape(half, packed)
    theirs = dot(pieces, weight_ref[...], 1, 0).astype(BF16)
    out_ref[pl.ds(pl.multiple_of(core_ref[0] * half, half), half), :] = mine_ref[...]
    out_ref[pl.ds(pl.multiple_of((1 - core_ref[0]) * half, half), half), :] = theirs


def weights_kernel(
    core_ref,
    own_ref,
    other_ref,
    hidden_ref,
    own_block_ref,
    other_block_ref,
    gate_ref,
    up_ref,
    down_ref,
):
    columns, width = gate_ref.shape
    half = own_ref.shape[0] * own_ref.shape[1]
    core = core_ref[0]
    own = own_ref[...].reshape(half, 2 * columns)
    other = other_ref[...].reshape(half, 2 * columns)
    own_hidden = hidden_ref[:, core].reshape(half, columns)
    other_hidden = hidden_ref[:, 1 - core].reshape(half, columns)
    own_block = own_block_ref[:, core].reshape(half, 2 * width)
    own_inputs, own_cotangent = own_block[:, :width], own_block[:, width:]
    other_block = other_block_ref[...].reshape(half, 2 * width)
    other_inputs, other_cotangent = other_block[:, :width], other_block[:, width:]
    packed = dot(own, own_inputs, 0, 0) + dot(other, other_inputs, 0, 0)
    gate_ref[...] = packed[:columns].astype(BF16)
    up_ref[...] = packed[columns:].astype(BF16)
    down_ref[...] = (
        dot(own_hidden, own_cotangent, 0, 0)
        + dot(other_hidden, other_cotangent, 0, 0)
    ).astype(BF16)


def total_kernel(core_ref, parts_ref, out_ref):
    out_ref[...] = jnp.sum(parts_ref[...].astype(F32), axis=0).astype(BF16)


def build(sizes):
    ny, nc, nh, nl, nx = sizes
    nz = nh * nl

    def on_device(inputs, w_gate, w_up, w_down, cotangent):
        width, columns = w_gate.shape
        rows = inputs.shape[0]
        part = nl * rows
        half = part * nx
        share_rows = half // ny
        core = lax.axis_index("c")
        both = jnp.concatenate([inputs, cotangent], axis=1)
        along_z = lax.all_gather(both, ("h", "l", "c"), axis=0, tiled=True)
        along_z = along_z.reshape(nh, nl, nc, rows, 2 * width)
        kept = lax.dynamic_index_in_dim(along_z, core, 0, False)
        kept = kept.swapaxes(0, 1).reshape(nc, part, 2 * width)

        w_gate, w_up, w_down = (after(w, along_z) for w in (w_gate, w_up, w_down))
        own_gate_up = jnp.concatenate([w_gate.T, w_up.T], axis=0)
        sib_gate_up, sib_down = sibling(own_gate_up), sibling(w_down)
        block = lax.all_to_all(jnp.broadcast_to(kept[None], (nx, *kept.shape)), "x", 0, 0)
        sums = local(
            sums_kernel,
            jax.ShapeDtypeStruct((ny, share_rows // 2, 6 * columns), BF16),
            12 * half * width * columns,
            8 * half * width + 12 * columns * width + 6 * half * columns,
            core,
            block,
            own_gate_up,
            sib_gate_up,
            fetched=(w_down, sib_down),
        )
        sums = lax.all_to_all(sums, "y", 0, 0)
        pieces, hidden = local(
            activations_kernel,
            (
                jax.ShapeDtypeStruct((ny, share_rows, 2 * columns), BF16),
                jax.ShapeDtypeStruct((share_rows, columns), BF16),
            ),
            20 * share_rows * columns,
            10 * half * columns,
            core,
            sums,
        )
        pieces = lax.all_to_all(pieces, "y", 0, 0)

        other_pieces = sibling(pieces)
        flops = 4 * half * width * columns
        moved = 4 * half * columns + 2 * half * width + 4 * columns * width
        mine = local(
            share_kernel,
            jax.ShapeDtypeStruct((half, width), BF16),
            flops,
            moved,
            core,
            pieces,
            own_gate_up,
        )
        shares = local(
            shares_kernel,
            pltpu.HBM((2 * half, width), BF16),
            flops,
            moved + 4 * half * width,
            core,
            mine,
            other_pieces,
            own_gate_up,
        )
        parts = lax.all_to_all(
            shares.reshape(nz * nx, rows, width), ("h", "x", "l"), 0, 0
        )
        grad_inputs = local(
            total_kernel,
            jax.ShapeDtypeStruct((rows, width), BF16),
            2 * half * width,
            4 * half * width,
            core,
            parts,
        )

        gradient = jax.ShapeDtypeStruct((columns, width), BF16)
        grad_gate, grad_up, grad_down = local(
            weights_kernel,
            (gradient, gradient, gradient),
            12 * half * width * columns,
            12 * half * columns + 8 * half * width + 6 * columns * width,
            core,
            pieces,
            other_pieces,
            lax.all_gather(after(hidden, shares), ("y", "c"), axis=0, tiled=True).reshape(
                ny, nc, share_rows, columns
            ),
            block,
            sibling(lax.dynamic_index_in_dim(after(block, shares), 1 - core, 1, False)),
        )
        return grad_inputs, grad_gate.T, grad_up.T, grad_down

    return on_device


def solution(mesh):
    row, col = mesh.devices.shape
    sizes = (row // 2, 2, 2, col // 8, 4)
    fine = Mesh(mesh.devices.reshape(sizes), ("y", "c", "h", "l", "x"))
    token_width = P(("h", "l", "x"), ("y", "c"))
    width_hidden = P(("y", "c"), ("h", "l", "x"))
    return jax.shard_map(
        build(sizes),
        mesh=fine,
        in_specs=(token_width, width_hidden, width_hidden, token_width, token_width),
        out_specs=(token_width, width_hidden, width_hidden, token_width),
        check_vma=False,
    )
```

```python
import functools

import jax
import jax.numpy as jnp
from jax import lax
from jax.experimental import pallas as pl
from jax.experimental.pallas import tpu as pltpu
from jax.sharding import Mesh, PartitionSpec as P

F32 = jnp.float32
BF16 = jnp.bfloat16
SWAP = [(0, 1), (1, 0)]


def dot(left, right, left_dim, right_dim):
    return lax.dot_general(
        left, right, (((left_dim,), (right_dim,)), ((), ())), preferred_element_type=F32
    )


def sibling(value):
    return lax.ppermute(value, "c", SWAP)


def after(value, *earlier):
    return lax.optimization_barrier((value, *earlier))[0]


def local(kernel, out_shape, flops, moved, core, *operands, fetched=()):
    scratch = [pltpu.VMEM(value.shape, value.dtype) for value in fetched]
    if fetched:
        scratch.append(pltpu.SemaphoreType.DMA((len(fetched),)))
    spaces = [pltpu.SMEM] + [pltpu.VMEM] * len(operands) + [pltpu.HBM] * len(fetched)
    return pl.pallas_call(
        kernel,
        out_shape=out_shape,
        in_specs=[pl.BlockSpec(memory_space=space) for space in spaces],
        out_specs=jax.tree.map(lambda _: pl.BlockSpec(memory_space=pltpu.VMEM), out_shape),
        scratch_shapes=scratch,
        compiler_params=pltpu.CompilerParams(vmem_limit_bytes=12 * 1024 * 1024),
        cost_estimate=pl.CostEstimate(flops=flops, bytes_accessed=moved, transcendentals=0),
    )(
        core.reshape(1).astype(jnp.int32),
        *operands,
        *(pltpu.with_memory_space_constraint(value, pltpu.HBM) for value in fetched),
    )


def sums_kernel(
    core_ref,
    block_ref,
    own_ref,
    sib_ref,
    own_down_hbm,
    sib_down_hbm,
    out_ref,
    own_down_ref,
    sib_down_ref,
    semaphores,
):
    own_copy = pltpu.make_async_copy(own_down_hbm, own_down_ref, semaphores.at[0])
    sib_copy = pltpu.make_async_copy(sib_down_hbm, sib_down_ref, semaphores.at[1])
    own_copy.start()
    sib_copy.start()
    core = core_ref[0]
    packed, width = own_ref.shape
    half = block_ref.shape[0] * block_ref.shape[2]
    own = block_ref[:, core].reshape(half, 2 * width)
    sib = block_ref[:, 1 - core].reshape(half, 2 * width)
    ny, rows, _ = out_ref.shape

    def store(sums, start):
        count = sums.shape[1]
        pairs = sums.reshape(ny, 2 * rows, count)
        out_ref[:, :, start : start + count] = pairs[:, :rows].astype(BF16)
        out_ref[:, :, start + count : start + 2 * count] = pairs[:, rows:].astype(BF16)

    store(dot(own[:, :width], own_ref[...], 1, 1) + dot(sib[:, :width], sib_ref[...], 1, 1), 0)
    own_copy.wait()
    sib_copy.wait()
    back = dot(own[:, width:], own_down_ref[...], 1, 1)
    store(back + dot(sib[:, width:], sib_down_ref[...], 1, 1), 2 * packed)


def sigmoid(value):
    small = jnp.exp(-jnp.abs(value))
    return jnp.where(value >= 0.0, 1.0, small) / (1.0 + small)


def activations_kernel(core_ref, parts_ref, out_ref, hidden_ref):
    columns = hidden_ref.shape[1]
    sums = jnp.sum(parts_ref[...].astype(F32), axis=0)
    gate_up = jnp.concatenate([sums[:, : 2 * columns], sums[:, 2 * columns : 4 * columns]], axis=0)
    gate_sum = gate_up[:, :columns]
    up_sum = gate_up[:, columns:]
    grad_hidden = jnp.concatenate(
        [sums[:, 4 * columns : 5 * columns], sums[:, 5 * columns :]], axis=0
    )
    sigmoid_gate = sigmoid(gate_sum)
    activated = gate_sum * sigmoid_gate
    grad_gate_act = grad_hidden * up_sum * sigmoid_gate * (1.0 + gate_sum * (1.0 - sigmoid_gate))
    out_ref[0, :, :columns] = grad_gate_act.astype(BF16)
    out_ref[0, :, columns:] = (grad_hidden * activated).astype(BF16)
    for k in range(1, out_ref.shape[0]):
        out_ref[k] = out_ref[0]
    hidden_ref[...] = (activated * up_sum).astype(BF16)


def share_kernel(flip, core_ref, pieces_ref, weight_ref, *refs):
    out_hbm, share_ref, semaphores = refs[-3:]
    half = share_ref.shape[0]
    part = half // 2
    side = 1 - core_ref[0] if flip else core_ref[0]
    pieces = pieces_ref[...].reshape(half, weight_ref.shape[0])
    copies = []
    for k in range(2):
        at = pl.ds(k * part, part)
        share_ref[at, :] = dot(pieces[k * part : (k + 1) * part], weight_ref[...], 1, 0).astype(BF16)
        start = pl.multiple_of(side * half + k * part, part)
        copies.append(
            pltpu.make_async_copy(
                share_ref.at[at], out_hbm.at[pl.ds(start, part)], semaphores.at[k]
            )
        )
        copies[-1].start()
    for copy in copies:
        copy.wait()


def weights_kernel(
    core_ref,
    own_ref,
    other_ref,
    hidden_ref,
    own_block_ref,
    other_block_ref,
    gate_ref,
    up_ref,
    down_ref,
):
    columns, width = gate_ref.shape
    half = own_ref.shape[0] * own_ref.shape[1]
    core = core_ref[0]
    own = own_ref[...].reshape(half, 2 * columns)
    other = other_ref[...].reshape(half, 2 * columns)
    own_hidden = hidden_ref[:, core].reshape(half, columns)
    other_hidden = hidden_ref[:, 1 - core].reshape(half, columns)
    own_block = own_block_ref[:, core].reshape(half, 2 * width)
    own_inputs, own_cotangent = own_block[:, :width], own_block[:, width:]
    other_block = other_block_ref[...].reshape(half, 2 * width)
    other_inputs, other_cotangent = other_block[:, :width], other_block[:, width:]
    packed = dot(own, own_inputs, 0, 0) + dot(other, other_inputs, 0, 0)
    gate_ref[...] = packed[:columns].astype(BF16)
    up_ref[...] = packed[columns:].astype(BF16)
    down_ref[...] = (
        dot(own_hidden, own_cotangent, 0, 0)
        + dot(other_hidden, other_cotangent, 0, 0)
    ).astype(BF16)


def total_kernel(core_ref, parts_ref, out_ref):
    out_ref[...] = jnp.sum(parts_ref[...].astype(F32), axis=0).astype(BF16)


def build(sizes):
    ny, nc, nh, nl, nx = sizes
    nz = nh * nl

    def on_device(inputs, w_gate, w_up, w_down, cotangent):
        width, columns = w_gate.shape
        rows = inputs.shape[0]
        part = nl * rows
        half = part * nx
        share_rows = half // ny
        core = lax.axis_index("c")
        both = jnp.concatenate([inputs, cotangent], axis=1)
        along_z = lax.all_gather(both, ("h", "l", "c"), axis=0, tiled=True)
        along_z = along_z.reshape(nh, nl, nc, rows, 2 * width)
        kept = lax.dynamic_index_in_dim(along_z, core, 0, False)
        kept = kept.swapaxes(0, 1).reshape(nc, part, 2 * width)

        w_gate, w_up, w_down = (after(w, along_z) for w in (w_gate, w_up, w_down))
        own_gate_up = jnp.concatenate([w_gate.T, w_up.T], axis=0)
        sib_gate_up, sib_down = sibling(own_gate_up), sibling(w_down)
        block = lax.all_to_all(jnp.broadcast_to(kept[None], (nx, *kept.shape)), "x", 0, 0)
        sums = local(
            sums_kernel,
            jax.ShapeDtypeStruct((ny, share_rows // 2, 6 * columns), BF16),
            12 * half * width * columns,
            8 * half * width + 12 * columns * width + 6 * half * columns,
            core,
            block,
            own_gate_up,
            sib_gate_up,
            fetched=(w_down, sib_down),
        )
        sums = lax.all_to_all(sums, "y", 0, 0)
        pieces, hidden = local(
            activations_kernel,
            (
                jax.ShapeDtypeStruct((ny, share_rows, 2 * columns), BF16),
                jax.ShapeDtypeStruct((share_rows, columns), BF16),
            ),
            20 * share_rows * columns,
            10 * half * columns,
            core,
            sums,
        )
        pieces = lax.all_to_all(pieces, "y", 0, 0)

        other_pieces = sibling(pieces)

        def share(flip, tokens, *written):
            return pl.pallas_call(
                functools.partial(share_kernel, flip),
                out_shape=pltpu.HBM((2 * half, width), BF16),
                in_specs=[pl.BlockSpec(memory_space=pltpu.SMEM)]
                + [pl.BlockSpec(memory_space=pltpu.VMEM)] * 2
                + [pl.BlockSpec(memory_space=pltpu.HBM)] * len(written),
                out_specs=pl.BlockSpec(memory_space=pltpu.HBM),
                input_output_aliases={3: 0} if written else {},
                scratch_shapes=[pltpu.VMEM((half, width), BF16), pltpu.SemaphoreType.DMA((2,))],
                compiler_params=pltpu.CompilerParams(vmem_limit_bytes=12 * 1024 * 1024),
                cost_estimate=pl.CostEstimate(
                    flops=4 * half * width * columns,
                    bytes_accessed=4 * half * columns + 2 * half * width + 4 * columns * width,
                    transcendentals=0,
                ),
            )(core.reshape(1).astype(jnp.int32), tokens, own_gate_up, *written)

        shares = share(True, other_pieces, share(False, pieces))
        parts = lax.all_to_all(
            shares.reshape(nz * nx, rows, width), ("h", "x", "l"), 0, 0
        )
        grad_inputs = local(
            total_kernel,
            jax.ShapeDtypeStruct((rows, width), BF16),
            2 * half * width,
            4 * half * width,
            core,
            parts,
        )

        gradient = jax.ShapeDtypeStruct((columns, width), BF16)
        grad_gate, grad_up, grad_down = local(
            weights_kernel,
            (gradient, gradient, gradient),
            12 * half * width * columns,
            12 * half * columns + 8 * half * width + 6 * columns * width,
            core,
            pieces,
            other_pieces,
            lax.all_gather(after(hidden, shares), ("y", "c"), axis=0, tiled=True).reshape(
                ny, nc, share_rows, columns
            ),
            block,
            sibling(lax.dynamic_index_in_dim(after(block, shares), 1 - core, 1, False)),
        )
        return grad_inputs, grad_gate.T, grad_up.T, grad_down

    return on_device


def solution(mesh):
    row, col = mesh.devices.shape
    sizes = (row // 2, 2, 2, col // 8, 4)
    fine = Mesh(mesh.devices.reshape(sizes), ("y", "c", "h", "l", "x"))
    token_width = P(("h", "l", "x"), ("y", "c"))
    width_hidden = P(("y", "c"), ("h", "l", "x"))
    return jax.shard_map(
        build(sizes),
        mesh=fine,
        in_specs=(token_width, width_hidden, width_hidden, token_width, token_width),
        out_specs=(token_width, width_hidden, width_hidden, token_width),
        check_vma=False,
    )
```

```python
import jax
import jax.numpy as jnp
from jax import lax
from jax.experimental import pallas as pl
from jax.experimental.pallas import tpu as pltpu
from jax.sharding import Mesh, PartitionSpec as P

F32 = jnp.float32
BF16 = jnp.bfloat16
SWAP = [(0, 1), (1, 0)]


def dot(left, right, left_dim, right_dim):
    return lax.dot_general(
        left, right, (((left_dim,), (right_dim,)), ((), ())), preferred_element_type=F32
    )


def sibling(value):
    return lax.ppermute(value, "c", SWAP)


def after(value, *earlier):
    return lax.optimization_barrier((value, *earlier))[0]


def local(kernel, out_shape, flops, moved, core, *operands, fetched=()):
    scratch = [pltpu.VMEM(value.shape, value.dtype) for value in fetched]
    if fetched:
        scratch.append(pltpu.SemaphoreType.DMA((len(fetched),)))
    spaces = [pltpu.SMEM] + [pltpu.VMEM] * len(operands) + [pltpu.HBM] * len(fetched)
    return pl.pallas_call(
        kernel,
        out_shape=out_shape,
        in_specs=[pl.BlockSpec(memory_space=space) for space in spaces],
        out_specs=jax.tree.map(lambda _: pl.BlockSpec(memory_space=pltpu.VMEM), out_shape),
        scratch_shapes=scratch,
        compiler_params=pltpu.CompilerParams(vmem_limit_bytes=16 * 1024 * 1024),
        cost_estimate=pl.CostEstimate(flops=flops, bytes_accessed=moved, transcendentals=0),
    )(
        core.reshape(1).astype(jnp.int32),
        *operands,
        *(pltpu.with_memory_space_constraint(value, pltpu.HBM) for value in fetched),
    )


def sums_kernel(
    core_ref,
    block_ref,
    own_ref,
    sib_ref,
    own_down_hbm,
    sib_down_hbm,
    out_ref,
    own_down_ref,
    sib_down_ref,
    semaphores,
):
    own_copy = pltpu.make_async_copy(own_down_hbm, own_down_ref, semaphores.at[0])
    sib_copy = pltpu.make_async_copy(sib_down_hbm, sib_down_ref, semaphores.at[1])
    own_copy.start()
    sib_copy.start()
    core = core_ref[0]
    packed, width = own_ref.shape
    half = block_ref.shape[0] * block_ref.shape[3]
    own, own_co = (block_ref[:, core, k].reshape(half, width) for k in range(2))
    sib, sib_co = (block_ref[:, 1 - core, k].reshape(half, width) for k in range(2))
    ny, rows, _ = out_ref.shape

    def store(sums, start):
        count = sums.shape[1]
        pairs = sums.reshape(ny, 2 * rows, count)
        out_ref[:, :, start : start + count] = pairs[:, :rows].astype(BF16)
        out_ref[:, :, start + count : start + 2 * count] = pairs[:, rows:].astype(BF16)

    store(dot(own, own_ref[...], 1, 1) + dot(sib, sib_ref[...], 1, 1), 0)
    own_copy.wait()
    sib_copy.wait()
    back = dot(own_co, own_down_ref[...], 1, 1)
    store(back + dot(sib_co, sib_down_ref[...], 1, 1), 2 * packed)


def sigmoid(value):
    small = jnp.exp(-jnp.abs(value))
    return jnp.where(value >= 0.0, 1.0, small) / (1.0 + small)


def activations_kernel(core_ref, parts_ref, out_ref, hidden_ref):
    columns = hidden_ref.shape[1]
    sums = jnp.sum(parts_ref[...].astype(F32), axis=0)
    gate_up = jnp.concatenate([sums[:, : 2 * columns], sums[:, 2 * columns : 4 * columns]], axis=0)
    gate_sum = gate_up[:, :columns]
    up_sum = gate_up[:, columns:]
    grad_hidden = jnp.concatenate(
        [sums[:, 4 * columns : 5 * columns], sums[:, 5 * columns :]], axis=0
    )
    sigmoid_gate = sigmoid(gate_sum)
    activated = gate_sum * sigmoid_gate
    grad_gate_act = grad_hidden * up_sum * sigmoid_gate * (1.0 + gate_sum * (1.0 - sigmoid_gate))
    out_ref[0, :, :columns] = grad_gate_act.astype(BF16)
    out_ref[0, :, columns:] = (grad_hidden * activated).astype(BF16)
    for k in range(1, out_ref.shape[0]):
        out_ref[k] = out_ref[0]
    hidden_ref[...] = (activated * up_sum).astype(BF16)


def share_kernel(core_ref, pieces_ref, weight_ref, out_ref):
    packed = pieces_ref.shape[2]
    pieces = pieces_ref[...].reshape(out_ref.shape[0], packed)
    out_ref[...] = dot(pieces, weight_ref[...], 1, 0).astype(BF16)


def shares_kernel(core_ref, mine_ref, pieces_ref, weight_ref, out_ref):
    half = mine_ref.shape[0]
    packed = pieces_ref.shape[2]
    pieces = pieces_ref[...].reshape(half, packed)
    theirs = dot(pieces, weight_ref[...], 1, 0).astype(BF16)
    out_ref[pl.ds(pl.multiple_of(core_ref[0] * half, half), half), :] = mine_ref[...]
    out_ref[pl.ds(pl.multiple_of((1 - core_ref[0]) * half, half), half), :] = theirs


def weights_kernel(
    core_ref,
    own_ref,
    other_ref,
    hidden_ref,
    own_block_ref,
    other_block_ref,
    gate_ref,
    up_ref,
    down_ref,
):
    columns, width = gate_ref.shape
    half = own_ref.shape[0] * own_ref.shape[1]
    core = core_ref[0]
    own = own_ref[...].reshape(half, 2 * columns)
    other = other_ref[...].reshape(half, 2 * columns)
    own_hidden = hidden_ref[:, core].reshape(half, columns)
    other_hidden = hidden_ref[:, 1 - core].reshape(half, columns)
    own_inputs, own_cotangent = (
        own_block_ref[:, core, k].reshape(half, width) for k in range(2)
    )
    other_inputs, other_cotangent = (
        other_block_ref[:, k].reshape(half, width) for k in range(2)
    )
    packed = dot(own, own_inputs, 0, 0) + dot(other, other_inputs, 0, 0)
    gate_ref[...] = packed[:columns].astype(BF16)
    up_ref[...] = packed[columns:].astype(BF16)
    down_ref[...] = (
        dot(own_hidden, own_cotangent, 0, 0)
        + dot(other_hidden, other_cotangent, 0, 0)
    ).astype(BF16)


def total_kernel(core_ref, parts_ref, out_ref):
    out_ref[...] = jnp.sum(parts_ref[...].astype(F32), axis=0).astype(BF16)


def build(sizes):
    ny, nc, nh, nl, nx = sizes
    nz = nh * nl

    def on_device(inputs, w_gate, w_up, w_down, cotangent):
        width, columns = w_gate.shape
        rows = inputs.shape[0]
        part = nl * rows
        half = part * nx
        share_rows = half // ny
        core = lax.axis_index("c")
        both = jnp.concatenate([inputs, cotangent], axis=0)
        along_z = lax.all_gather(both, ("h", "l", "c"), axis=0, tiled=True)
        along_z = along_z.reshape(nh, nl, nc, 2, rows, width)
        kept = lax.dynamic_index_in_dim(along_z, core, 0, False)
        kept = kept.transpose(1, 2, 0, 3, 4).reshape(nc, 2, part, width)

        w_gate, w_up, w_down = (after(w, along_z) for w in (w_gate, w_up, w_down))
        own_gate_up = jnp.concatenate([w_gate.T, w_up.T], axis=0)
        sib_gate_up, sib_down = sibling(own_gate_up), sibling(w_down)
        block = lax.all_to_all(jnp.broadcast_to(kept[None], (nx, *kept.shape)), "x", 0, 0)
        sums = local(
            sums_kernel,
            jax.ShapeDtypeStruct((ny, share_rows // 2, 6 * columns), BF16),
            12 * half * width * columns,
            8 * half * width + 12 * columns * width + 6 * half * columns,
            core,
            block,
            own_gate_up,
            sib_gate_up,
            fetched=(w_down, sib_down),
        )
        sums = lax.all_to_all(sums, "y", 0, 0)
        pieces, hidden = local(
            activations_kernel,
            (
                jax.ShapeDtypeStruct((ny, share_rows, 2 * columns), BF16),
                jax.ShapeDtypeStruct((share_rows, columns), BF16),
            ),
            20 * share_rows * columns,
            10 * half * columns,
            core,
            sums,
        )
        pieces = lax.all_to_all(pieces, "y", 0, 0)

        other_pieces = sibling(pieces)
        flops = 4 * half * width * columns
        moved = 4 * half * columns + 2 * half * width + 4 * columns * width
        mine = local(
            share_kernel,
            jax.ShapeDtypeStruct((half, width), BF16),
            flops,
            moved,
            core,
            pieces,
            own_gate_up,
        )
        shares = local(
            shares_kernel,
            pltpu.HBM((2 * half, width), BF16),
            flops,
            moved + 4 * half * width,
            core,
            mine,
            other_pieces,
            own_gate_up,
        )
        parts = lax.all_to_all(
            shares.reshape(nz * nx, rows, width), ("h", "x", "l"), 0, 0
        )
        grad_inputs = local(
            total_kernel,
            jax.ShapeDtypeStruct((rows, width), BF16),
            2 * half * width,
            4 * half * width,
            core,
            parts,
        )

        gradient = jax.ShapeDtypeStruct((columns, width), BF16)
        grad_gate, grad_up, grad_down = local(
            weights_kernel,
            (gradient, gradient, gradient),
            12 * half * width * columns,
            12 * half * columns + 8 * half * width + 6 * columns * width,
            core,
            pieces,
            other_pieces,
            lax.all_gather(after(hidden, shares), ("y", "c"), axis=0, tiled=True).reshape(
                ny, nc, share_rows, columns
            ),
            block,
            sibling(lax.dynamic_index_in_dim(after(block, shares), 1 - core, 1, False)),
        )
        return grad_inputs, grad_gate.T, grad_up.T, grad_down

    return on_device


def solution(mesh):
    row, col = mesh.devices.shape
    sizes = (row // 2, 2, 2, col // 8, 4)
    fine = Mesh(mesh.devices.reshape(sizes), ("y", "c", "h", "l", "x"))
    token_width = P(("h", "l", "x"), ("y", "c"))
    width_hidden = P(("y", "c"), ("h", "l", "x"))
    return jax.shard_map(
        build(sizes),
        mesh=fine,
        in_specs=(token_width, width_hidden, width_hidden, token_width, token_width),
        out_specs=(token_width, width_hidden, width_hidden, token_width),
        check_vma=False,
    )
```
